256 devices in a mesh: section: 16 (over y, x), ctx: 16 (over z, core).
Axes of the slice: x: 4, y: 4, z: 8, core: 2. Of those that a mesh axis runs over, the one named last changes fastest.
Arguments:
- query_fwd: bfloat16 [16, 2048, 4096], P('section', 'ctx'), may hold values from -100 to 100
- key_fwd: bfloat16 [16, 2048, 512], P('section', 'ctx'), may hold values from -4.5 to 4.5
- value_fwd: bfloat16 [16, 2048, 512], P('section', 'ctx'), may hold values from -6 to 6
- doc_len_fwd: int32 [16, 16], P('section'), may hold values from 1 to 384, 2048 in all within a row
- query_bwd: bfloat16 [16, 2048, 4096], P('section', 'ctx'), may hold values from -100 to 100
- key_bwd: bfloat16 [16, 2048, 512], P('section', 'ctx'), may hold values from -4.5 to 4.5
- value_bwd: bfloat16 [16, 2048, 512], P('section', 'ctx'), may hold values from -6 to 6
- doc_len_bwd: int32 [16, 16], P('section'), may hold values from 1 to 384, 2048 in all within a row
- grad_held: bfloat16 [16, 2048, 4096], P('section', 'ctx'), may hold values from -6 to 6
Outputs:
- next_stream: bfloat16 [16, 2048, 4096], P('section', 'ctx')
- grad_query: bfloat16 [16, 2048, 4096], P('section', 'ctx')
- grad_key: bfloat16 [16, 2048, 512], P('section', 'ctx')
- grad_value: bfloat16 [16, 2048, 512], P('section', 'ctx')
The draws below stay inside these ranges and needn't reach their ends.
Inputs may be any that keep to these rules, and one draw needn't show every extreme that they name: `doc_len_fwd`: each row holds the 16 document lengths of one packed micro-batch in order, summing to 2048; the longest is exactly 384. `doc_len_bwd`: each row holds the 16 document lengths of one packed micro-batch in order, summing to 2048; the longest is exactly 384.
All inputs are finite; a program needn't handle non-finite values.
Results may differ from the reference program's by a relative error of at most 0.007.
Values may be sent and summed in bfloat16 or wider, within the bound.
No kernel may reach another device: no remote copies, remote signals or barrier semaphores. Data moves between devices by JAX's collectives and lax.ppermute only.
A program may use at most 64 MiB of HBM per device.

```python
import math
import jax
import jax.numpy as jnp
import numpy as np
from jax import lax

HEADS = 32
KV_HEADS = 4
HEAD_DIM = 128
TOK_DEV = 128
DOCS = 16
TOKENS = 2048
SECTIONS = 16
MOST = 384


def aligned_pair(key, strength):
    group_size = HEADS // KV_HEADS
    key_rows = jax.random.truncated_normal(jax.random.fold_in(key, 11), -4.5, 4.5, (SECTIONS, TOKENS, KV_HEADS, HEAD_DIM), jnp.float32)
    query_rows = jax.random.truncated_normal(jax.random.fold_in(key, 12), -4.5, 4.5, (SECTIONS, TOKENS, HEADS, HEAD_DIM), jnp.float32)
    positions = jnp.arange(TOKENS)
    chosen = jnp.where(positions % 32 == 17, strength, 0.0)
    amplitude = 12.0 + 5.0 * (positions // 32 % 3).astype(jnp.float32)
    before = jnp.roll(chosen, -1)
    following = jnp.roll(key_rows, -1, axis=1)
    key_rows = key_rows * (1.0 - before)[None, :, None, None] + (before * 0.99)[None, :, None, None] * following
    repeated = jnp.repeat(key_rows, group_size, axis=2)
    query_rows = query_rows * (1.0 - chosen)[None, :, None, None] + (chosen * amplitude)[None, :, None, None] * repeated
    return (query_rows.reshape(SECTIONS, TOKENS, HEADS * HEAD_DIM), key_rows.reshape(SECTIONS, TOKENS, KV_HEADS * HEAD_DIM))


def draw_query_fwd(key, part):
    strength = 0.0
    return aligned_pair(jax.random.fold_in(key, 1), strength)[0].astype(jnp.bfloat16)


def draw_key_fwd(key, part):
    strength = 0.0
    return aligned_pair(jax.random.fold_in(key, 1), strength)[1].astype(jnp.bfloat16)


def draw_query_bwd(key, part):
    strength = 0.0
    return aligned_pair(jax.random.fold_in(key, 2), strength)[0].astype(jnp.bfloat16)


def draw_key_bwd(key, part):
    strength = 0.0
    return aligned_pair(jax.random.fold_in(key, 2), strength)[1].astype(jnp.bfloat16)


def block_scale(stream_key, extent, cuts, smallest, high):
    factor_of = 1.0
    for axis_at, shards_of in cuts:
        draws = jax.random.uniform(jax.random.fold_in(jax.random.fold_in(stream_key, 6), axis_at), (shards_of,), jnp.float32, smallest / len(cuts), high / len(cuts))
        factor_of = factor_of * jnp.repeat(jnp.exp(draws), extent[axis_at] // shards_of).reshape((-1,) + (1,) * (len(extent) - 1 - axis_at))
    return factor_of


def split_up(number_of, total, bound, skew):
    portions = [(1 << 20) // math.isqrt(rank ** skew) + 1 for rank in range(2, number_of + 1)]
    spare, counts = total - bound - (number_of - 1), [1] * (number_of - 1)
    while spare > 0:
        candidates = [i for i in range(number_of - 1) if counts[i] < bound]
        pool, remaining = sum([portions[i] for i in candidates]), spare
        for i in candidates:
            addition = min(bound - counts[i], max(1, remaining * portions[i] // pool), spare)
            counts[i] = counts[i] + addition
            spare = spare - addition
    return np.array([bound] + counts)


def ragged_sizes(rng, count, total, limit, skew):
    if count == 2:
        one = jax.random.randint(rng, (), max(1, total - limit), min(limit, total - 1) + 1)
        return jnp.stack([one, total - one])
    tallies = jnp.asarray(split_up(count, total, limit, skew), jnp.int32)
    pairs = (count - 1) // 2
    donor, sink = tallies[1:1 + 2 * pairs:2], tallies[2:2 + 2 * pairs:2]
    margin = jnp.minimum(donor - 1, limit - sink)
    shifted = jax.random.randint(jax.random.fold_in(rng, 1), (pairs,), 0, 1 << 20) % (margin + 1)
    tallies = tallies.at[1:1 + 2 * pairs:2].set(donor - shifted).at[2:2 + 2 * pairs:2].set(sink + shifted)
    return tallies[jax.random.permutation(jax.random.fold_in(rng, 2), count)]


def gaussian(own_key, dims, spread, bound, split=(), kind=jnp.bfloat16):
    result = jax.random.normal(own_key, dims, jnp.float32) * spread
    if len(split) > 0:
        result = block_scale(own_key, dims, split, -0.22, 0.18) * result
    return jnp.clip(result, min=-bound, max=bound).astype(kind)


def setup_inputs(seed: int = 0) -> dict:
    key_of = jax.random.split(jax.random.key(seed), 10)
    return {
        "query_fwd": draw_query_fwd(jax.random.fold_in(key_of[9], 71), 0),
        "key_fwd": draw_key_fwd(jax.random.fold_in(key_of[9], 71), 0),
        "value_fwd": gaussian(key_of[2], (SECTIONS, TOKENS, KV_HEADS * HEAD_DIM), 1.0, 6.0, ((0, 16), (1, 16))),
        "doc_len_fwd": jax.vmap(lambda own: ragged_sizes(own, DOCS, TOKENS, MOST, 2))(jax.random.split(key_of[3], SECTIONS)).reshape((SECTIONS, DOCS)).astype(jnp.int32),
        "query_bwd": draw_query_bwd(jax.random.fold_in(key_of[9], 71), 0),
        "key_bwd": draw_key_bwd(jax.random.fold_in(key_of[9], 71), 0),
        "value_bwd": gaussian(key_of[6], (SECTIONS, TOKENS, KV_HEADS * HEAD_DIM), 1.0, 6.0, ((0, 16), (1, 16))),
        "doc_len_bwd": jax.vmap(lambda own: ragged_sizes(own, DOCS, TOKENS, MOST, 2))(jax.random.split(key_of[7], SECTIONS)).reshape((SECTIONS, DOCS)).astype(jnp.int32),
        "grad_held": gaussian(key_of[8], (SECTIONS, TOKENS, HEADS * HEAD_DIM), 1.0, 6.0, ((0, 16), (1, 16))),
    }


MASKED_SCORE = -1e30


def doc_index(lengths, positions):
    doc_ends = jnp.cumsum(lengths)
    return jnp.sum((positions[:, None] >= doc_ends[None, :]).astype(jnp.int32), axis=1)


def section_mask(lengths):
    positions = jnp.arange(TOKENS, dtype=jnp.int32)
    doc_ids = doc_index(lengths, positions)
    return (doc_ids[:, None] == doc_ids[None, :]) & (positions[None, :] <= positions[:, None])


def group_weights(queries, key_rows, allowed):
    scores = jnp.einsum("qhd,kd->hqk", queries.astype(jnp.float32), key_rows.astype(jnp.float32)) * HEAD_DIM ** -0.5
    scores = jnp.where(allowed[None], scores, MASKED_SCORE)
    row_max = jnp.max(scores, axis=-1, keepdims=True)
    weights = jnp.where(allowed[None], jnp.exp(scores - row_max), 0.0)
    return weights, jnp.sum(weights, axis=-1)


def forward_section(operands):
    query, key_rows, value_rows, lengths = operands
    allowed = section_mask(lengths)
    group_size = HEADS // KV_HEADS
    query_four = query.reshape(TOKENS, KV_HEADS, group_size, HEAD_DIM)
    key_three = key_rows.reshape(TOKENS, KV_HEADS, HEAD_DIM)
    value_three = value_rows.reshape(TOKENS, KV_HEADS, HEAD_DIM)
    outputs = []
    for kv_group in range(KV_HEADS):
        weights, totals = group_weights(query_four[:, kv_group], key_three[:, kv_group], allowed)
        rounded = lax.optimization_barrier(weights.astype(jnp.bfloat16)).astype(jnp.float32)
        mixed = jnp.einsum("hqk,kd->qhd", rounded, value_three[:, kv_group].astype(jnp.float32))
        outputs.append(mixed / totals.T[:, :, None])
    return jnp.stack(outputs, axis=1).reshape(TOKENS, HEADS * HEAD_DIM).astype(jnp.bfloat16)


def backward_section(operands):
    query, key_rows, value_rows, lengths, out_grad = operands
    allowed = section_mask(lengths)
    group_size = HEADS // KV_HEADS
    blocks = TOKENS // TOK_DEV
    scale = HEAD_DIM ** -0.5
    query_four = query.reshape(TOKENS, KV_HEADS, group_size, HEAD_DIM)
    grad_four = out_grad.reshape(TOKENS, KV_HEADS, group_size, HEAD_DIM)
    key_three = key_rows.reshape(TOKENS, KV_HEADS, HEAD_DIM)
    value_three = value_rows.reshape(TOKENS, KV_HEADS, HEAD_DIM)
    query_grads, key_grads, value_grads = [], [], []
    for kv_group in range(KV_HEADS):
        weights, totals = group_weights(query_four[:, kv_group], key_three[:, kv_group], allowed)
        probabilities = weights / totals[..., None]
        d_prob = jnp.einsum("qhd,kd->hqk", grad_four[:, kv_group].astype(jnp.float32), value_three[:, kv_group].astype(jnp.float32))
        row_delta = jnp.sum(probabilities * d_prob, axis=-1, keepdims=True)
        d_score = lax.optimization_barrier((probabilities * (d_prob - row_delta)).astype(jnp.bfloat16)).astype(jnp.float32)
        low_probs = lax.optimization_barrier(probabilities.astype(jnp.bfloat16)).astype(jnp.float32)
        query_grads.append(jnp.einsum("hqk,kd->qhd", d_score, key_three[:, kv_group].astype(jnp.float32)) * scale)
        score_blocks = d_score.reshape(group_size, blocks, TOK_DEV, TOKENS)
        prob_blocks = low_probs.reshape(group_size, blocks, TOK_DEV, TOKENS)
        query_blocks = query_four[:, kv_group].astype(jnp.float32).reshape(blocks, TOK_DEV, group_size, HEAD_DIM)
        grad_blocks = grad_four[:, kv_group].astype(jnp.float32).reshape(blocks, TOK_DEV, group_size, HEAD_DIM)
        key_part = jnp.einsum("hcrk,crhd->ckd", score_blocks, query_blocks) * scale
        value_part = jnp.einsum("hcrk,crhd->ckd", prob_blocks, grad_blocks)
        key_grads.append(jnp.sum(lax.optimization_barrier(key_part.astype(jnp.bfloat16)).astype(jnp.float32), axis=0))
        value_grads.append(jnp.sum(lax.optimization_barrier(value_part.astype(jnp.bfloat16)).astype(jnp.float32), axis=0))
    grad_query = jnp.stack(query_grads, axis=1).reshape(TOKENS, HEADS * HEAD_DIM).astype(jnp.bfloat16)
    grad_key = jnp.stack(key_grads, axis=1).reshape(TOKENS, KV_HEADS * HEAD_DIM).astype(jnp.bfloat16)
    grad_value = jnp.stack(value_grads, axis=1).reshape(TOKENS, KV_HEADS * HEAD_DIM).astype(jnp.bfloat16)
    return grad_query, grad_key, grad_value


def reference(query_fwd, key_fwd, value_fwd, doc_len_fwd, query_bwd, key_bwd, value_bwd, doc_len_bwd, grad_held):
    attended = lax.map(forward_section, (query_fwd, key_fwd, value_fwd, doc_len_fwd))
    next_stream = jnp.concatenate([jnp.zeros_like(attended[:1]), attended[:-1]], axis=0)
    out_grad = jnp.concatenate([grad_held[1:], jnp.zeros_like(grad_held[:1])], axis=0)
    grad_query, grad_key, grad_value = lax.map(backward_section, (query_bwd, key_bwd, value_bwd, doc_len_bwd, out_grad))
    return next_stream, grad_query, grad_key, grad_value
```

```python
import math

import jax
import jax.numpy as jnp
from jax import lax
from jax.experimental import pallas as pl
from jax.experimental.pallas import tpu as pltpu
from jax.sharding import PartitionSpec as P

HEADS = 32
KV_HEADS = 4
GROUP = HEADS // KV_HEADS
HEAD_DIM = 128
REACH = 3
ROWS = 128
KEYS = (REACH + 1) * ROWS
DOCS = 16
SCALE = HEAD_DIM**-0.5
SCALE_LOG2 = SCALE * math.log2(math.e)
MASKED = -1e30
KV_WIDTH = KV_HEADS * HEAD_DIM
GROUP_WIDTH = GROUP * HEAD_DIM
CHUNKS = (2, 2)
VMEM = 48 * 1024 * 1024
NT = (((1,), (1,)), ((), ()))


def from_behind(value, axis, steps, what="moved"):
    count = lax.axis_size(axis)
    with jax.named_scope(what):
        return lax.ppermute(value, axis, [(at, (at + steps) % count) for at in range(count)])


def after(*values):
    return lax.optimization_barrier(values)


def params():
    return pltpu.CompilerParams(vmem_limit_bytes=VMEM)


def cost(flops, bytes_accessed):
    return pl.CostEstimate(flops=flops, bytes_accessed=bytes_accessed, transcendentals=0)


def fill_bias(place_ref, len_ref, bias_ref):
    base = (place_ref[0] - REACH) * ROWS
    key = base + lax.broadcasted_iota(jnp.int32, (KEYS, ROWS), 0)
    query = base + REACH * ROWS + lax.broadcasted_iota(jnp.int32, (8, ROWS), 1)
    start = jnp.zeros((8, ROWS), jnp.int32)
    end = jnp.int32(0)
    for doc in range(DOCS):
        end = end + len_ref[0, doc]
        start = jnp.where(query >= end, end, start)
    bias = jnp.where((key >= start[:1]) & (key <= query[:1]), 0.0, MASKED)
    bias_ref[:, :ROWS] = bias
    bias_ref[:, ROWS:] = bias


def two_heads(ref, pair):
    at = 2 * pair * HEAD_DIM
    return jnp.concatenate(
        [ref[0, :, at : at + HEAD_DIM], ref[0, :, at + HEAD_DIM : at + 2 * HEAD_DIM]], axis=0
    )


def weights_of(keys, queries, bias_ref):
    scores = lax.dot_general(keys, queries, NT, preferred_element_type=jnp.float32)
    scores = scores + bias_ref[...]
    top = jnp.max(scores, axis=0, keepdims=True)
    weights = jnp.exp2((scores - top) * SCALE_LOG2)
    return weights, 1.0 / jnp.sum(weights, axis=0, keepdims=True)


def put_heads(out_ref, pair, flipped):
    at = 2 * pair * HEAD_DIM
    out_ref[0, :, at : at + HEAD_DIM] = flipped[:, :ROWS].T.astype(jnp.bfloat16)
    out_ref[0, :, at + HEAD_DIM : at + 2 * HEAD_DIM] = flipped[:, ROWS:].T.astype(jnp.bfloat16)


def stacked(refs):
    return jnp.concatenate([ref[0] for ref in refs], axis=0)


def forward_kernel(place_ref, len_ref, query_ref, *refs):
    key_refs, value_refs, (out_ref, bias_ref) = refs[:4], refs[4:8], refs[8:]

    @pl.when(pl.program_id(0) == 0)
    def _():
        fill_bias(place_ref, len_ref, bias_ref)

    keep = place_ref[1].astype(jnp.float32)
    keys = stacked(key_refs)
    values_t = stacked(value_refs).T
    for pair in range(GROUP // 2):
        weights, inverse = weights_of(keys, two_heads(query_ref, pair), bias_ref)
        mixed = jnp.dot(
            values_t, weights.astype(jnp.bfloat16), preferred_element_type=jnp.float32
        )
        put_heads(out_ref, pair, mixed * (inverse * keep))


def backward_kernel(place_ref, len_ref, query_ref, grad_ref, *refs):
    key_refs, value_refs = refs[:4], refs[4:8]
    out_ref, own_ref, middle_ref, pair_ref, bias_ref = refs[-5:]

    @pl.when(pl.program_id(0) == 0)
    def _():
        fill_bias(place_ref, len_ref, bias_ref)

    keep = place_ref[2].astype(jnp.bfloat16)
    keys, values = stacked(key_refs), stacked(value_refs)
    keys_t = keys.T
    key_sum = value_sum = None
    for pair in range(GROUP // 2):
        queries, grads = two_heads(query_ref, pair), two_heads(grad_ref, pair) * keep
        weights, inverse = weights_of(keys, queries, bias_ref)
        d_prob = lax.dot_general(values, grads, NT, preferred_element_type=jnp.float32)
        probs = weights * inverse
        delta = jnp.sum(probs * d_prob, axis=0, keepdims=True)
        d_score = (probs * (d_prob - delta)).astype(jnp.bfloat16)
        key_term = jnp.dot(d_score, queries, preferred_element_type=jnp.float32)
        value_term = jnp.dot(
            probs.astype(jnp.bfloat16), grads, preferred_element_type=jnp.float32
        )
        key_sum = key_term if key_sum is None else key_sum + key_term
        value_sum = value_term if value_sum is None else value_sum + value_term
        d_query = jnp.dot(keys_t, d_score, preferred_element_type=jnp.float32)
        put_heads(out_ref, pair, d_query * SCALE)
    places = ((pair_ref, 1), (middle_ref, 0), (pair_ref, 0), (own_ref, 0))
    for piece, (part_ref, lead) in enumerate(places):
        at = slice(piece * ROWS, (piece + 1) * ROWS)
        part_ref[lead, :, :HEAD_DIM] = (key_sum[at] * SCALE).astype(jnp.bfloat16)
        part_ref[lead, :, HEAD_DIM:] = value_sum[at].astype(jnp.bfloat16)


def group_spec(first):
    return pl.BlockSpec((1, ROWS, GROUP_WIDTH), lambda i: (0, 0, first + i))


def common_specs(first):
    smem = pl.BlockSpec(memory_space=pltpu.SMEM)
    specs = []
    for col in (first, KV_HEADS + first):
        for lead in (1, 0, 0, 0):
            specs.append(
                pl.BlockSpec(
                    (1, ROWS, HEAD_DIM), lambda i, lead=lead, col=col: (lead, 0, col + i)
                )
            )
    return [smem, smem], specs


def in_order(own, middle, pair):
    return [pair, middle, pair, own] * 2


def forward(place, lengths, query, pieces):
    scalars, heads = common_specs(0)
    return pl.pallas_call(
        forward_kernel,
        grid=(KV_HEADS,),
        out_shape=jax.ShapeDtypeStruct(query.shape, jnp.bfloat16),
        in_specs=scalars + [group_spec(0)] + heads,
        out_specs=group_spec(0),
        scratch_shapes=[pltpu.VMEM((KEYS, 2 * ROWS), jnp.float32)],
        cost_estimate=cost(4 * HEADS * ROWS * KEYS * HEAD_DIM, 3 << 20),
        compiler_params=params(),
    )(place, lengths, query, *in_order(*pieces))


def backward(place, lengths, query, out_grad, pieces, first, so_far):
    groups = out_grad.shape[2] // GROUP_WIDTH
    width = groups * 2 * HEAD_DIM
    leads = (1, 1, 2)
    scalars, heads = common_specs(first)
    in_specs = scalars + [group_spec(first), group_spec(0)] + heads
    operands = [place, lengths, query, out_grad, *in_order(*pieces)]
    aliases = {}
    if so_far is not None:
        in_specs.append(pl.BlockSpec(memory_space=pl.ANY))
        aliases = {len(operands): 0}
        operands.append(so_far)
    result = pl.pallas_call(
        backward_kernel,
        grid=(groups,),
        out_shape=[jax.ShapeDtypeStruct(query.shape, jnp.bfloat16)]
        + [jax.ShapeDtypeStruct((lead, ROWS, width), jnp.bfloat16) for lead in leads],
        in_specs=in_specs,
        out_specs=[group_spec(first)]
        + [pl.BlockSpec((lead, ROWS, 2 * HEAD_DIM), lambda i: (0, 0, i)) for lead in leads],
        scratch_shapes=[pltpu.VMEM((KEYS, 2 * ROWS), jnp.float32)],
        input_output_aliases=aliases,
        cost_estimate=cost(10 * groups * GROUP * ROWS * KEYS * HEAD_DIM, groups << 20),
        compiler_params=params(),
    )(*operands)
    return result[0], result[1:]


def add_kernel(*refs):
    part_refs, (key_ref, value_ref) = refs[:-2], refs[-2:]
    first = 0
    for chunk, groups in enumerate(CHUNKS):
        total = part_refs[3 * chunk][0].astype(jnp.float32)
        for ref in part_refs[3 * chunk + 1 : 3 * chunk + 3]:
            total = total + ref[0].astype(jnp.float32)
        total = total.astype(jnp.bfloat16)
        for group in range(groups):
            at, to = 2 * group * HEAD_DIM, (first + group) * HEAD_DIM
            key_ref[0, :, to : to + HEAD_DIM] = total[:, at : at + HEAD_DIM]
            value_ref[0, :, to : to + HEAD_DIM] = total[:, at + HEAD_DIM : at + 2 * HEAD_DIM]
        first += groups


def add_parts(parts):
    shape = jax.ShapeDtypeStruct((1, ROWS, KV_WIDTH), jnp.bfloat16)
    return pl.pallas_call(
        add_kernel,
        out_shape=[shape, shape],
        grid=(1,),
        in_specs=[
            pl.BlockSpec((1,) + part.shape[1:], lambda i: (0, 0, 0)) for part in parts
        ],
        out_specs=[pl.BlockSpec(shape.shape, lambda i: (0, 0, 0))] * 2,
        cost_estimate=cost(0, 2 << 20),
        compiler_params=params(),
    )(*parts)


def on_device(
    query_fwd,
    key_fwd,
    value_fwd,
    doc_len_fwd,
    query_bwd,
    key_bwd,
    value_bwd,
    doc_len_bwd,
    grad_held,
):
    section = lax.axis_index("section")
    last = lax.axis_size("section") - 1
    place = jnp.stack([lax.axis_index("ctx"), section > 0, section < last]).astype(jnp.int32)
    starts = [sum(CHUNKS[:chunk]) for chunk in range(len(CHUNKS) + 1)]
    grads = [
        grad_held[:, :, at * GROUP_WIDTH : to * GROUP_WIDTH]
        for at, to in zip(starts[:-1], starts[1:])
    ]
    key_fwd, key_bwd, grads[0] = after(key_fwd, key_bwd, grads[0])
    out_grads = [
        from_behind(grad, "section", -1, f"grad_{chunk}") for chunk, grad in enumerate(grads)
    ]
    own_fwd = from_behind(
        jnp.concatenate([key_fwd, value_fwd], axis=2), "section", 1, "kv_moved"
    )
    len_moved = from_behind(doc_len_fwd, "section", 1, "len_moved")
    own_bwd = jnp.concatenate([key_bwd, value_bwd], axis=2)
    middle_bwd = from_behind(own_bwd, "ctx", 2, "kv_bwd_middle")
    query_fwd, own_fwd, len_moved = after(query_fwd, own_fwd, len_moved)
    query_moved = from_behind(query_fwd, "section", 1, "query_moved")
    middle_fwd = from_behind(own_fwd, "ctx", 2, "kv_fwd_middle")
    pair_bwd = from_behind(
        jnp.concatenate([own_bwd, middle_bwd], axis=0), "ctx", 1, "kv_bwd_pair"
    )
    middle_fwd, pair_bwd = after(middle_fwd, pair_bwd)
    pair_fwd = from_behind(
        jnp.concatenate([own_fwd, middle_fwd], axis=0), "ctx", 1, "kv_fwd_pair"
    )
    grad_query = None
    parts = []
    for chunk, out_grad in enumerate(out_grads):
        grad_query, (own, middle, pair) = backward(
            place,
            doc_len_bwd,
            query_bwd,
            out_grad,
            (own_bwd, middle_bwd, pair_bwd),
            starts[chunk],
            grad_query,
        )
        if chunk > 0:
            pair, parts[-1], query_moved = after(pair, parts[-1], query_moved)
        pair = from_behind(pair, "ctx", -1, f"part_pair_{chunk}")
        middle = (middle.astype(jnp.float32) + pair[1:].astype(jnp.float32)).astype(jnp.bfloat16)
        parts += [own, pair, from_behind(middle, "ctx", -2, f"part_middle_{chunk}")]
    next_stream = forward(place, len_moved, query_moved, (own_fwd, middle_fwd, pair_fwd))
    next_stream, *parts = after(next_stream, *parts)
    grad_key, grad_value = add_parts(parts)
    return (next_stream, grad_query, grad_key, grad_value)


def solution(mesh):
    spec = P("section", "ctx", None)
    row = P("section", None)
    return jax.shard_map(
        on_device,
        mesh=mesh,
        in_specs=(spec, spec, spec, row, spec, spec, spec, row, spec),
        out_specs=(spec, spec, spec, spec),
        check_vma=False,
    )
```

```python
import math

import jax
import jax.numpy as jnp
from jax import lax
from jax.experimental import pallas as pl
from jax.experimental.pallas import tpu as pltpu
from jax.sharding import PartitionSpec as P

HEADS = 32
KV_HEADS = 4
GROUP = HEADS // KV_HEADS
HEAD_DIM = 128
REACH = 3
ROWS = 128
KEYS = (REACH + 1) * ROWS
DOCS = 16
SCALE = HEAD_DIM**-0.5
SCALE_LOG2 = SCALE * math.log2(math.e)
MASKED = -1e30
KV_WIDTH = KV_HEADS * HEAD_DIM
GROUP_WIDTH = GROUP * HEAD_DIM
CHUNKS = (4,)
FOLDS = ((0,),)
HEADS_AT_ONCE = 4
VMEM = 24 * 1024 * 1024
COST = 1
PACK_COST = 1
PACK_VMEM = 56 * 1024 * 1024
SMALL_VMEM = 8 * 1024 * 1024
NT = (((1,), (1,)), ((), ()))


def from_behind(value, axis, steps, what="moved"):
    count = lax.axis_size(axis)
    with jax.named_scope(what):
        return lax.ppermute(value, axis, [(at, (at + steps) % count) for at in range(count)])


def swapped(value, what):
    count = lax.axis_size("ctx")
    with jax.named_scope(what):
        return lax.ppermute(value, "ctx", [(at, at ^ 1) for at in range(count)])


def second_core():
    return lax.rem(lax.axis_index("ctx"), 2) == 1


def after(value, *earlier):
    return lax.optimization_barrier((value, *earlier))[0]


def params(limit):
    return pltpu.CompilerParams(vmem_limit_bytes=limit)


def cost(flops, bytes_accessed):
    return pl.CostEstimate(flops=flops, bytes_accessed=bytes_accessed, transcendentals=0)


def first_keys(len_ref, columns):
    shard = lax.axis_index("ctx")
    query = shard * ROWS + lax.broadcasted_iota(jnp.int32, (ROWS, columns), 0)
    start = jnp.zeros((ROWS, columns), jnp.int32)
    end = jnp.int32(0)
    for doc in range(DOCS):
        end = end + len_ref[0, doc]
        start = jnp.where(query >= end, end, start)
    return start - (shard - REACH) * ROWS


def fill_bias(first, bias_ref):
    query = REACH * ROWS + lax.broadcasted_iota(jnp.int32, (ROWS, ROWS), 0)
    for piece in range(REACH + 1):
        key = piece * ROWS + lax.broadcasted_iota(jnp.int32, (ROWS, ROWS), 1)
        seen = (key >= first) & (key <= query)
        bias_ref[:, piece * ROWS : (piece + 1) * ROWS] = jnp.where(seen, 0.0, MASKED)


def head(index):
    return slice(index * HEAD_DIM, (index + 1) * HEAD_DIM)


def weights_of(queries, keys, bias):
    scores = lax.dot_general(queries, keys, NT, preferred_element_type=jnp.float32) + bias
    top = jnp.max(scores, axis=1, keepdims=True)
    return jnp.exp2((scores - top) * SCALE_LOG2)


def stacked(refs):
    return jnp.concatenate([ref[0] for ref in refs], axis=0)


def stack_heads(ref, first, count):
    return jnp.concatenate([ref[0, :, head(first + index)] for index in range(count)], axis=0)


def forward_kernel(first_ref, query_ref, *refs):
    key_refs, value_refs, (out_ref, bias_ref) = refs[:4], refs[4:8], refs[8:]

    @pl.when(pl.program_id(0) == 0)
    def _():
        high, low = (first_ref[0, :, at : at + 1].astype(jnp.float32) for at in (0, 64))
        fill_bias((high * 256.0 + low).astype(jnp.int32), bias_ref)

    keep = (lax.axis_index("section") > 0).astype(jnp.float32)
    keys = stacked(key_refs)
    values = jnp.concatenate(
        [stacked(value_refs), jnp.ones((KEYS, HEAD_DIM), jnp.bfloat16)], axis=1
    )
    for index in range(GROUP):
        weights = weights_of(query_ref[0, :, head(index)], keys, bias_ref[...])
        mixed = jnp.dot(weights.astype(jnp.bfloat16), values, preferred_element_type=jnp.float32)
        result = mixed[:, :HEAD_DIM] * keep / mixed[:, HEAD_DIM:]
        out_ref[0, :, head(index)] = result.astype(jnp.bfloat16)


def probs_kernel(len_ref, query_ref, *refs):
    key_refs, (out_ref, bias_ref) = refs[:4], refs[4:]

    @pl.when(pl.program_id(0) == 0)
    def _():
        fill_bias(first_keys(len_ref, ROWS), bias_ref)

    keys = stacked(key_refs)
    for first in range(0, GROUP, HEADS_AT_ONCE):
        queries = stack_heads(query_ref, first, HEADS_AT_ONCE)
        weights = weights_of(queries, keys, jnp.concatenate([bias_ref[...]] * HEADS_AT_ONCE, axis=0))
        total = jnp.sum(weights, axis=1, keepdims=True)
        out_ref[0, first * ROWS : (first + HEADS_AT_ONCE) * ROWS, :] = weights * (1.0 / total)


def backward_kernel(probs_ref, query_ref, grad_ref, *refs):
    key_refs, value_refs = refs[:4], refs[4:8]
    (
        out_ref, own_ref, middle_ref, near_ref, far_ref, queries_ref, grads_ref, scores_ref, low_ref
    ) = refs[-9:]
    last = lax.axis_size("section") - 1
    keep = (lax.axis_index("section") < last).astype(jnp.float32).astype(jnp.bfloat16)
    keys, values = stacked(key_refs), stacked(value_refs)
    queries_ref[...] = stack_heads(query_ref, 0, GROUP)
    grads_ref[...] = stack_heads(grad_ref, 0, GROUP) * keep
    for first in range(0, GROUP, HEADS_AT_ONCE):
        at = slice(first * ROWS, (first + HEADS_AT_ONCE) * ROWS)
        probs = probs_ref[0, at, :]
        d_prob = lax.dot_general(grads_ref[at, :], values, NT, preferred_element_type=jnp.float32)
        delta = jnp.sum(probs * d_prob, axis=1, keepdims=True)
        scores_ref[at, :] = (probs * (d_prob - delta)).astype(jnp.bfloat16)
        low_ref[at, :] = probs.astype(jnp.bfloat16)
    d_query = jnp.dot(scores_ref[...], keys, preferred_element_type=jnp.float32) * SCALE
    for index in range(GROUP):
        out_ref[0, :, head(index)] = d_query[index * ROWS : (index + 1) * ROWS].astype(
            jnp.bfloat16
        )
    d_key = jnp.dot(queries_ref[...].T, scores_ref[...], preferred_element_type=jnp.float32).T
    d_value = jnp.dot(grads_ref[...].T, low_ref[...], preferred_element_type=jnp.float32).T
    for piece, part_ref in enumerate((far_ref, middle_ref, near_ref, own_ref)):
        at = slice(piece * ROWS, (piece + 1) * ROWS)
        part_ref[0, :, :HEAD_DIM] = (d_key[at] * SCALE).astype(jnp.bfloat16)
        part_ref[0, :, HEAD_DIM:] = d_value[at].astype(jnp.bfloat16)


def small_call(
    kernel, operands, in_specs, shapes, out_specs, steps, limit=SMALL_VMEM, bytes_accessed=COST
):
    return pl.pallas_call(
        kernel,
        grid=(steps,),
        out_shape=[jax.ShapeDtypeStruct(shape, jnp.bfloat16) for shape in shapes],
        in_specs=in_specs,
        out_specs=out_specs,
        cost_estimate=cost(COST, bytes_accessed),
        compiler_params=params(limit),
    )(*operands)


def row_spec(width, steps, column=0):
    return pl.BlockSpec((1, ROWS // steps, width), lambda i: (0, i, column))


def pack_kernel(len_ref, key_fwd, value_fwd, key_bwd, value_bwd, fwd_ref, bwd_ref):
    for key_ref, value_ref, out_ref in (
        (key_fwd, value_fwd, fwd_ref),
        (key_bwd, value_bwd, bwd_ref),
    ):
        out_ref[0, :, :KV_WIDTH] = key_ref[0]
        out_ref[0, :, KV_WIDTH : 2 * KV_WIDTH] = value_ref[0]
    first = first_keys(len_ref, ROWS)
    high = jnp.where(first >= 256, 1, 0)
    left = lax.broadcasted_iota(jnp.int32, (ROWS, ROWS), 1) < ROWS // 2
    coded = jnp.where(left, high, first - 256 * high)
    fwd_ref[0, :, 2 * KV_WIDTH :] = coded.astype(jnp.float32).astype(jnp.bfloat16)


def pack(lengths, *keys_and_values):
    widths = [2 * KV_WIDTH + ROWS, 2 * KV_WIDTH]
    return small_call(
        pack_kernel,
        (lengths, *keys_and_values),
        [pl.BlockSpec(memory_space=pltpu.SMEM)] + [row_spec(KV_WIDTH, 1)] * 4,
        [(1, ROWS, width) for width in widths],
        [row_spec(width, 1) for width in widths],
        1,
        PACK_VMEM,
        PACK_COST,
    )


def folded(middles, fars, nears):
    sums = []
    for middle, far, near in zip(middles, fars, nears):
        total = middle.astype(jnp.float32) + far.astype(jnp.float32)
        total = total + jnp.where(second_core(), near.astype(jnp.float32), 0.0)
        sums.append(total.astype(jnp.bfloat16))
    return sums[0] if len(sums) == 1 else jnp.concatenate(sums, axis=2)


def group_spec(first):
    return pl.BlockSpec((1, ROWS, GROUP_WIDTH), lambda i: (0, 0, first + i))


def key_specs(first):
    return [pl.BlockSpec((1, ROWS, HEAD_DIM), lambda i: (0, 0, first + i))] * 4


def value_specs(first):
    return key_specs(KV_HEADS + first)


def forward(query, pieces):
    return pl.pallas_call(
        forward_kernel,
        grid=(KV_HEADS,),
        out_shape=jax.ShapeDtypeStruct(query.shape, jnp.bfloat16),
        in_specs=[
            pl.BlockSpec((1, ROWS, ROWS), lambda i: (0, 0, 2 * KV_HEADS)),
            group_spec(0),
        ]
        + key_specs(0)
        + value_specs(0),
        out_specs=group_spec(0),
        scratch_shapes=[pltpu.VMEM((ROWS, KEYS), jnp.float32)],
        cost_estimate=cost(COST, COST),
        compiler_params=params(VMEM),
    )(pieces[-1], query, *pieces, *pieces)


def probabilities(lengths, query, pieces):
    block = (1, GROUP * ROWS, KEYS)
    return pl.pallas_call(
        probs_kernel,
        grid=(KV_HEADS,),
        out_shape=jax.ShapeDtypeStruct((KV_HEADS,) + block[1:], jnp.float32),
        in_specs=[pl.BlockSpec(memory_space=pltpu.SMEM), group_spec(0)] + key_specs(0),
        out_specs=pl.BlockSpec(block, lambda i: (i, 0, 0)),
        scratch_shapes=[pltpu.VMEM((ROWS, KEYS), jnp.float32)],
        cost_estimate=cost(COST, COST),
        compiler_params=params(VMEM),
    )(lengths, query, *pieces)


def backward(probs, query, out_grad, pieces, first, groups, so_far):
    width = groups * 2 * HEAD_DIM
    in_specs = [pl.BlockSpec((1, GROUP * ROWS, KEYS), lambda i: (first + i, 0, 0))]
    in_specs += [group_spec(first)] * 2 + key_specs(first) + value_specs(first)
    operands = [probs, query, out_grad, *pieces, *pieces]
    aliases = {}
    if so_far is not None:
        in_specs.append(pl.BlockSpec(memory_space=pl.ANY))
        aliases = {len(operands): 0}
        operands.append(so_far)
    result = pl.pallas_call(
        backward_kernel,
        grid=(groups,),
        out_shape=[jax.ShapeDtypeStruct(query.shape, jnp.bfloat16)]
        + [jax.ShapeDtypeStruct((1, ROWS, width), jnp.bfloat16)] * 4,
        in_specs=in_specs,
        out_specs=[group_spec(first)]
        + [pl.BlockSpec((1, ROWS, 2 * HEAD_DIM), lambda i: (0, 0, i))] * 4,
        scratch_shapes=[
            pltpu.VMEM((GROUP * ROWS, HEAD_DIM), jnp.bfloat16),
            pltpu.VMEM((GROUP * ROWS, HEAD_DIM), jnp.bfloat16),
            pltpu.VMEM((GROUP * ROWS, KEYS), jnp.bfloat16),
            pltpu.VMEM((GROUP * ROWS, KEYS), jnp.bfloat16),
        ],
        input_output_aliases=aliases,
        cost_estimate=cost(COST, COST),
        compiler_params=params(VMEM),
    )(*operands)
    return result[0], result[1:]


def add_kernel(*refs):
    chunks = len(CHUNKS)
    own_refs, near_refs, fold_refs = refs[:chunks], refs[chunks : 2 * chunks], refs[2 * chunks : -2]
    key_ref, value_ref = refs[-2:]
    folds = [
        (ref, at)
        for ref, members in zip(fold_refs, FOLDS)
        for at in [sum(CHUNKS[chunk] for chunk in members[:spot]) for spot in range(len(members))]
    ]
    first = 0
    first_core = lax.rem(lax.axis_index("ctx"), 2) == 0
    for groups, own_ref, near_ref, (fold_ref, at) in zip(CHUNKS, own_refs, near_refs, folds):
        for group in range(groups):
            here = slice(2 * group * HEAD_DIM, 2 * (group + 1) * HEAD_DIM)
            there = slice(2 * (at + group) * HEAD_DIM, 2 * (at + group + 1) * HEAD_DIM)
            total = own_ref[0, :, here].astype(jnp.float32)
            near = near_ref[0, :, here].astype(jnp.float32)
            total = total + jnp.where(first_core, near, 0.0)
            total = (total + fold_ref[0, :, there].astype(jnp.float32)).astype(jnp.bfloat16)
            key_ref[0, :, head(first + group)] = total[:, :HEAD_DIM]
            value_ref[0, :, head(first + group)] = total[:, HEAD_DIM:]
        first += groups


def add_parts(*parts):
    return small_call(
        add_kernel,
        parts,
        [row_spec(part.shape[2], 1) for part in parts],
        [(1, ROWS, KV_WIDTH)] * 2,
        [row_spec(KV_WIDTH, 1)] * 2,
        1,
    )


def gather_behind(own, what, *earlier):
    middle = from_behind(after(own, *earlier), "ctx", 2, what + "_middle")
    far = from_behind(middle, "ctx", 1, what + "_far")
    near = swapped(jnp.where(second_core(), middle, own), what + "_near")
    return far, middle, near, own


def on_device(
    query_fwd,
    key_fwd,
    value_fwd,
    doc_len_fwd,
    query_bwd,
    key_bwd,
    value_bwd,
    doc_len_bwd,
    grad_held,
):
    out_grad = from_behind(grad_held, "section", -1, "grad")
    kv_fwd, own_bwd = pack(doc_len_fwd, key_fwd, value_fwd, key_bwd, value_bwd)
    own_fwd = from_behind(kv_fwd, "section", 1, "kv_moved")
    pieces_bwd = gather_behind(own_bwd, "kv_bwd", kv_fwd)
    query_moved = from_behind(after(query_fwd, own_fwd), "section", 1, "query_moved")
    probs = probabilities(doc_len_bwd, query_bwd, pieces_bwd)
    pieces_fwd = gather_behind(own_fwd, "kv_fwd", probs)
    grad_query = None
    first = 0
    owns, middles, nears, fars, folds = [], [], [], [], []
    for chunk, groups in enumerate(CHUNKS):
        grad_query, (own, middle, near, far) = backward(
            probs, query_bwd, out_grad, pieces_bwd, first, groups, grad_query
        )
        first += groups
        if chunk > 0:
            far = after(far, fars[0])
        owns.append(own)
        middles.append(middle)
        fars.append(from_behind(far, "ctx", -1, f"part_far_{chunk}"))
        nears.append(swapped(near, f"part_near_{chunk}"))
    for members in FOLDS:
        fold = folded(*([values[chunk] for chunk in members] for values in (middles, fars, nears)))
        if members == FOLDS[-1]:
            fold = after(fold, query_moved)
        folds.append(from_behind(fold, "ctx", -2, f"part_fold_{members[0]}"))
    next_stream = forward(query_moved, pieces_fwd)
    grad_key, grad_value = add_parts(after(owns[0], next_stream), *owns[1:], *nears, *folds)
    return (next_stream, grad_query, grad_key, grad_value)


def solution(mesh):
    spec = P("section", "ctx", None)
    row = P("section", None)
    return jax.shard_map(
        on_device,
        mesh=mesh,
        in_specs=(spec, spec, spec, row, spec, spec, spec, row, spec),
        out_specs=(spec, spec, spec, spec),
        check_vma=False,
    )
```

```python
import math

import jax
import jax.numpy as jnp
from jax import lax
from jax.experimental import pallas as pl
from jax.experimental.pallas import tpu as pltpu
from jax.sharding import PartitionSpec as P

HEADS = 32
KV_HEADS = 4
GROUP = HEADS // KV_HEADS
HEAD_DIM = 128
REACH = 3
ROWS = 128
KEYS = (REACH + 1) * ROWS
DOCS = 16
SCALE = HEAD_DIM**-0.5
SCALE_LOG2 = SCALE * math.log2(math.e)
MASKED = -1e30
KV_WIDTH = KV_HEADS * HEAD_DIM
GROUP_WIDTH = GROUP * HEAD_DIM
HEADS_AT_ONCE = 4
VMEM = 24 * 1024 * 1024
COST = 1
PACK_COST = 1
PACK_VMEM = 56 * 1024 * 1024
SMALL_VMEM = 8 * 1024 * 1024
NT = (((1,), (1,)), ((), ()))


def from_behind(value, axis, steps, what="moved"):
    count = lax.axis_size(axis)
    with jax.named_scope(what):
        return lax.ppermute(value, axis, [(at, (at + steps) % count) for at in range(count)])


def swapped(value, what):
    count = lax.axis_size("ctx")
    with jax.named_scope(what):
        return lax.ppermute(value, "ctx", [(at, at ^ 1) for at in range(count)])


def second_core():
    return lax.rem(lax.axis_index("ctx"), 2) == 1


def after(value, *earlier):
    return lax.optimization_barrier((value, *earlier))[0]


def params(limit):
    return pltpu.CompilerParams(vmem_limit_bytes=limit)


def cost(flops, bytes_accessed):
    return pl.CostEstimate(flops=flops, bytes_accessed=bytes_accessed, transcendentals=0)


def first_keys(len_ref, columns):
    shard = lax.axis_index("ctx")
    query = shard * ROWS + lax.broadcasted_iota(jnp.int32, (ROWS, columns), 0)
    start = jnp.zeros((ROWS, columns), jnp.int32)
    end = jnp.int32(0)
    for doc in range(DOCS):
        end = end + len_ref[0, doc]
        start = jnp.where(query >= end, end, start)
    return start - (shard - REACH) * ROWS


def fill_bias(first, bias_ref):
    query = REACH * ROWS + lax.broadcasted_iota(jnp.int32, (ROWS, ROWS), 0)
    for piece in range(REACH + 1):
        key = piece * ROWS + lax.broadcasted_iota(jnp.int32, (ROWS, ROWS), 1)
        seen = (key >= first) & (key <= query)
        bias_ref[:, piece * ROWS : (piece + 1) * ROWS] = jnp.where(seen, 0.0, MASKED)


def head(index):
    return slice(index * HEAD_DIM, (index + 1) * HEAD_DIM)


def weights_of(queries, keys, bias):
    scores = lax.dot_general(queries, keys, NT, preferred_element_type=jnp.float32) + bias
    top = jnp.max(scores, axis=1, keepdims=True)
    return jnp.exp2((scores - top) * SCALE_LOG2)


def stacked(refs):
    return jnp.concatenate([ref[0] for ref in refs], axis=0)


def stack_heads(ref, first, count):
    return jnp.concatenate([ref[0, :, head(first + index)] for index in range(count)], axis=0)


def forward_kernel(first_ref, query_ref, *refs):
    key_refs, value_refs, (out_ref, bias_ref) = refs[:4], refs[4:8], refs[8:]

    @pl.when(pl.program_id(0) == 0)
    def _():
        high, low = (first_ref[0, :, at : at + 1].astype(jnp.float32) for at in (0, 64))
        fill_bias((high * 256.0 + low).astype(jnp.int32), bias_ref)

    keep = (lax.axis_index("section") > 0).astype(jnp.float32)
    keys = stacked(key_refs)
    values = jnp.concatenate(
        [stacked(value_refs), jnp.ones((KEYS, HEAD_DIM), jnp.bfloat16)], axis=1
    )
    for index in range(GROUP):
        weights = weights_of(query_ref[0, :, head(index)], keys, bias_ref[...])
        mixed = jnp.dot(weights.astype(jnp.bfloat16), values, preferred_element_type=jnp.float32)
        result = mixed[:, :HEAD_DIM] * keep / mixed[:, HEAD_DIM:]
        out_ref[0, :, head(index)] = result.astype(jnp.bfloat16)


def probs_kernel(len_ref, query_ref, *refs):
    key_refs, (out_ref, bias_ref) = refs[:4], refs[4:]

    @pl.when(pl.program_id(0) == 0)
    def _():
        fill_bias(first_keys(len_ref, ROWS), bias_ref)

    keys = stacked(key_refs)
    for first in range(0, GROUP, HEADS_AT_ONCE):
        queries = stack_heads(query_ref, first, HEADS_AT_ONCE)
        weights = weights_of(queries, keys, jnp.concatenate([bias_ref[...]] * HEADS_AT_ONCE, axis=0))
        total = jnp.sum(weights, axis=1, keepdims=True)
        out_ref[0, first * ROWS : (first + HEADS_AT_ONCE) * ROWS, :] = weights * (1.0 / total)


def backward_kernel(probs_ref, query_ref, grad_ref, *refs):
    key_refs, value_refs = refs[:4], refs[4:8]
    (
        scores_ref, own_ref, middle_ref, near_ref, far_ref, queries_ref, grads_ref, low_ref
    ) = refs[-8:]
    last = lax.axis_size("section") - 1
    keep = (lax.axis_index("section") < last).astype(jnp.float32).astype(jnp.bfloat16)
    keys, values = stacked(key_refs), stacked(value_refs)
    queries_ref[...] = stack_heads(query_ref, 0, GROUP)
    grads_ref[...] = stack_heads(grad_ref, 0, GROUP) * keep
    for first in range(0, GROUP, HEADS_AT_ONCE):
        at = slice(first * ROWS, (first + HEADS_AT_ONCE) * ROWS)
        probs = probs_ref[0, at, :]
        d_prob = lax.dot_general(grads_ref[at, :], values, NT, preferred_element_type=jnp.float32)
        delta = jnp.sum(probs * d_prob, axis=1, keepdims=True)
        scores_ref[0, at, :] = (probs * (d_prob - delta)).astype(jnp.bfloat16)
        low_ref[at, :] = probs.astype(jnp.bfloat16)
    d_key = jnp.dot(queries_ref[...].T, scores_ref[0], preferred_element_type=jnp.float32).T
    d_value = jnp.dot(grads_ref[...].T, low_ref[...], preferred_element_type=jnp.float32).T
    for piece, part_ref in enumerate((far_ref, middle_ref, near_ref, own_ref)):
        at = slice(piece * ROWS, (piece + 1) * ROWS)
        part_ref[0, :, :HEAD_DIM] = (d_key[at] * SCALE).astype(jnp.bfloat16)
        part_ref[0, :, HEAD_DIM:] = d_value[at].astype(jnp.bfloat16)


def query_kernel(scores_ref, *refs):
    key_refs, out_ref = refs[:4], refs[4]
    keys = stacked(key_refs)
    d_query = jnp.dot(scores_ref[0], keys, preferred_element_type=jnp.float32) * SCALE
    for index in range(GROUP):
        out_ref[0, :, head(index)] = d_query[index * ROWS : (index + 1) * ROWS].astype(
            jnp.bfloat16
        )


def small_call(
    kernel, operands, in_specs, shapes, out_specs, steps, limit=SMALL_VMEM, bytes_accessed=COST
):
    return pl.pallas_call(
        kernel,
        grid=(steps,),
        out_shape=[jax.ShapeDtypeStruct(shape, jnp.bfloat16) for shape in shapes],
        in_specs=in_specs,
        out_specs=out_specs,
        cost_estimate=cost(COST, bytes_accessed),
        compiler_params=params(limit),
    )(*operands)


def row_spec(width, steps, column=0):
    return pl.BlockSpec((1, ROWS // steps, width), lambda i: (0, i, column))


def pack_kernel(len_ref, key_fwd, value_fwd, key_bwd, value_bwd, fwd_ref, bwd_ref):
    for key_ref, value_ref, out_ref in (
        (key_fwd, value_fwd, fwd_ref),
        (key_bwd, value_bwd, bwd_ref),
    ):
        out_ref[0, :, :KV_WIDTH] = key_ref[0]
        out_ref[0, :, KV_WIDTH : 2 * KV_WIDTH] = value_ref[0]
    first = first_keys(len_ref, ROWS)
    high = jnp.where(first >= 256, 1, 0)
    left = lax.broadcasted_iota(jnp.int32, (ROWS, ROWS), 1) < ROWS // 2
    coded = jnp.where(left, high, first - 256 * high)
    fwd_ref[0, :, 2 * KV_WIDTH :] = coded.astype(jnp.float32).astype(jnp.bfloat16)


def pack(lengths, *keys_and_values):
    widths = [2 * KV_WIDTH + ROWS, 2 * KV_WIDTH]
    return small_call(
        pack_kernel,
        (lengths, *keys_and_values),
        [pl.BlockSpec(memory_space=pltpu.SMEM)] + [row_spec(KV_WIDTH, 1)] * 4,
        [(1, ROWS, width) for width in widths],
        [row_spec(width, 1) for width in widths],
        1,
        PACK_VMEM,
        PACK_COST,
    )


def folded(middle, far, near):
    total = middle.astype(jnp.float32) + far.astype(jnp.float32)
    total = total + jnp.where(second_core(), near.astype(jnp.float32), 0.0)
    return total.astype(jnp.bfloat16)


def group_spec(first):
    return pl.BlockSpec((1, ROWS, GROUP_WIDTH), lambda i: (0, 0, first + i))


def key_specs(first):
    return [pl.BlockSpec((1, ROWS, HEAD_DIM), lambda i: (0, 0, first + i))] * 4


def value_specs(first):
    return key_specs(KV_HEADS + first)


def forward(query, pieces):
    return pl.pallas_call(
        forward_kernel,
        grid=(KV_HEADS,),
        out_shape=jax.ShapeDtypeStruct(query.shape, jnp.bfloat16),
        in_specs=[
            pl.BlockSpec((1, ROWS, ROWS), lambda i: (0, 0, 2 * KV_HEADS)),
            group_spec(0),
        ]
        + key_specs(0)
        + value_specs(0),
        out_specs=group_spec(0),
        scratch_shapes=[pltpu.VMEM((ROWS, KEYS), jnp.float32)],
        cost_estimate=cost(COST, COST),
        compiler_params=params(VMEM),
    )(pieces[-1], query, *pieces, *pieces)


def probabilities(lengths, query, pieces):
    block = (1, GROUP * ROWS, KEYS)
    return pl.pallas_call(
        probs_kernel,
        grid=(KV_HEADS,),
        out_shape=jax.ShapeDtypeStruct((KV_HEADS,) + block[1:], jnp.float32),
        in_specs=[pl.BlockSpec(memory_space=pltpu.SMEM), group_spec(0)] + key_specs(0),
        out_specs=pl.BlockSpec(block, lambda i: (i, 0, 0)),
        scratch_shapes=[pltpu.VMEM((ROWS, KEYS), jnp.float32)],
        cost_estimate=cost(COST, COST),
        compiler_params=params(VMEM),
    )(lengths, query, *pieces)


def backward(probs, query, out_grad, pieces):
    block = (1, GROUP * ROWS, KEYS)
    return pl.pallas_call(
        backward_kernel,
        grid=(KV_HEADS,),
        out_shape=[jax.ShapeDtypeStruct(probs.shape, jnp.bfloat16)]
        + [jax.ShapeDtypeStruct((1, ROWS, 2 * KV_WIDTH), jnp.bfloat16)] * 4,
        in_specs=[pl.BlockSpec(block, lambda i: (i, 0, 0))]
        + [group_spec(0)] * 2
        + key_specs(0)
        + value_specs(0),
        out_specs=[pl.BlockSpec(block, lambda i: (i, 0, 0))]
        + [pl.BlockSpec((1, ROWS, 2 * HEAD_DIM), lambda i: (0, 0, i))] * 4,
        scratch_shapes=[
            pltpu.VMEM((GROUP * ROWS, HEAD_DIM), jnp.bfloat16),
            pltpu.VMEM((GROUP * ROWS, HEAD_DIM), jnp.bfloat16),
            pltpu.VMEM((GROUP * ROWS, KEYS), jnp.bfloat16),
        ],
        cost_estimate=cost(COST, COST),
        compiler_params=params(VMEM),
    )(probs, query, out_grad, *pieces, *pieces)


def query_gradient(scores, pieces):
    return pl.pallas_call(
        query_kernel,
        grid=(KV_HEADS,),
        out_shape=jax.ShapeDtypeStruct((1, ROWS, HEADS * HEAD_DIM), jnp.bfloat16),
        in_specs=[pl.BlockSpec((1, GROUP * ROWS, KEYS), lambda i: (i, 0, 0))] + key_specs(0),
        out_specs=group_spec(0),
        cost_estimate=cost(COST, COST),
        compiler_params=params(VMEM),
    )(scores, *pieces)


def add_kernel(own_ref, near_ref, fold_ref, key_ref, value_ref):
    first_core = lax.rem(lax.axis_index("ctx"), 2) == 0
    total = own_ref[0].astype(jnp.float32) + fold_ref[0].astype(jnp.float32)
    total = total + jnp.where(first_core, near_ref[0].astype(jnp.float32), 0.0)
    total = total.astype(jnp.bfloat16)
    for group in range(KV_HEADS):
        key_ref[0, :, head(group)] = total[:, head(2 * group)]
        value_ref[0, :, head(group)] = total[:, head(2 * group + 1)]


def add_parts(*parts):
    return small_call(
        add_kernel,
        parts,
        [row_spec(part.shape[2], 1) for part in parts],
        [(1, ROWS, KV_WIDTH)] * 2,
        [row_spec(KV_WIDTH, 1)] * 2,
        1,
    )


def gather_behind(own, what, *earlier):
    middle = from_behind(after(own, *earlier), "ctx", 2, what + "_middle")
    return from_behind(middle, "ctx", 1, what + "_far"), middle


def shared_behind(own, middle, what, *earlier):
    shared = jnp.where(second_core(), middle, own)
    return swapped(after(shared, *earlier), what + "_near")


def on_device(
    query_fwd,
    key_fwd,
    value_fwd,
    doc_len_fwd,
    query_bwd,
    key_bwd,
    value_bwd,
    doc_len_bwd,
    grad_held,
):
    out_grad = from_behind(grad_held, "section", -1, "grad")
    kv_fwd, own_bwd = pack(doc_len_fwd, key_fwd, value_fwd, key_bwd, value_bwd)
    own_fwd = from_behind(kv_fwd, "section", 1, "kv_moved")
    far_bwd, middle_bwd = gather_behind(own_bwd, "kv_bwd", kv_fwd)
    near_bwd = shared_behind(own_bwd, middle_bwd, "kv_bwd")
    pieces_bwd = (far_bwd, middle_bwd, near_bwd, own_bwd)
    query_moved = from_behind(after(query_fwd, own_fwd), "section", 1, "query_moved")
    probs = probabilities(doc_len_bwd, query_bwd, pieces_bwd)
    far_fwd, middle_fwd = gather_behind(own_fwd, "kv_fwd", probs, out_grad, own_fwd)
    scores, own, middle, near, far = backward(probs, query_bwd, out_grad, pieces_bwd)
    far = from_behind(far, "ctx", -1, "part_far")
    near = swapped(near, "part_near")
    grad_query = query_gradient(scores, pieces_bwd)
    fold = after(folded(middle, far, near), grad_query, query_moved)
    near_fwd = shared_behind(own_fwd, middle_fwd, "kv_fwd")
    fold = from_behind(fold, "ctx", -2, "part_fold")
    next_stream = forward(query_moved, (far_fwd, middle_fwd, near_fwd, own_fwd))
    grad_key, grad_value = add_parts(after(own, next_stream), near, fold)
    return (next_stream, grad_query, grad_key, grad_value)


def solution(mesh):
    spec = P("section", "ctx", None)
    row = P("section", None)
    return jax.shard_map(
        on_device,
        mesh=mesh,
        in_specs=(spec, spec, spec, row, spec, spec, spec, row, spec),
        out_specs=(spec, spec, spec, spec),
        check_vma=False,
    )
```

```python
import math

import jax
import jax.numpy as jnp
from jax import lax
from jax.experimental import pallas as pl
from jax.experimental.pallas import tpu as pltpu
from jax.sharding import PartitionSpec as P

HEADS = 32
KV_HEADS = 4
GROUP = HEADS // KV_HEADS
HEAD_DIM = 128
REACH = 3
ROWS = 128
KEYS = (REACH + 1) * ROWS
DOCS = 16
SCALE = HEAD_DIM**-0.5
SCALE_LOG2 = SCALE * math.log2(math.e)
MASKED = -1e30
KV_WIDTH = KV_HEADS * HEAD_DIM
GROUP_WIDTH = GROUP * HEAD_DIM
CHUNKS = (4,)
FOLDS = ((0,),)
HEADS_AT_ONCE = 4
VMEM = 24 * 1024 * 1024
COST = 1
PACK_COST = 1
PACK_STEPS = 2
PACK_VMEM = 56 * 1024 * 1024
SMALL_VMEM = 8 * 1024 * 1024
NT = (((1,), (1,)), ((), ()))


def from_behind(value, axis, steps, what="moved"):
    count = lax.axis_size(axis)
    with jax.named_scope(what):
        return lax.ppermute(value, axis, [(at, (at + steps) % count) for at in range(count)])


def swapped(value, what):
    count = lax.axis_size("ctx")
    with jax.named_scope(what):
        return lax.ppermute(value, "ctx", [(at, at ^ 1) for at in range(count)])


def second_core():
    return lax.rem(lax.axis_index("ctx"), 2) == 1


def after(value, *earlier):
    return lax.optimization_barrier((value, *earlier))[0]


def params(limit):
    return pltpu.CompilerParams(vmem_limit_bytes=limit)


def cost(flops, bytes_accessed):
    return pl.CostEstimate(flops=flops, bytes_accessed=bytes_accessed, transcendentals=0)


def first_keys(len_ref, rows=ROWS, offset=0):
    shard = lax.axis_index("ctx")
    query = shard * ROWS + offset + lax.broadcasted_iota(jnp.int32, (rows, ROWS), 0)
    start = jnp.zeros((rows, ROWS), jnp.int32)
    end = jnp.int32(0)
    for doc in range(DOCS):
        end = end + len_ref[0, doc]
        start = jnp.where(query >= end, end, start)
    return start - (shard - REACH) * ROWS


def fill_bias(first, bias_ref):
    query = REACH * ROWS + lax.broadcasted_iota(jnp.int32, (ROWS, ROWS), 0)
    for piece in range(REACH + 1):
        key = piece * ROWS + lax.broadcasted_iota(jnp.int32, (ROWS, ROWS), 1)
        seen = (key >= first) & (key <= query)
        bias_ref[:, piece * ROWS : (piece + 1) * ROWS] = jnp.where(seen, 0.0, MASKED)


def head(index):
    return slice(index * HEAD_DIM, (index + 1) * HEAD_DIM)


def weights_of(queries, keys, bias):
    scores = lax.dot_general(queries, keys, NT, preferred_element_type=jnp.float32) + bias
    top = jnp.max(scores, axis=1, keepdims=True)
    return jnp.exp2((scores - top) * SCALE_LOG2)


def stacked(refs):
    return jnp.concatenate([ref[0] for ref in refs], axis=0)


def stack_heads(ref, first, count):
    return jnp.concatenate([ref[0, :, head(first + index)] for index in range(count)], axis=0)


def forward_kernel(first_ref, query_ref, *refs):
    key_refs, value_refs, (out_ref, bias_ref) = refs[:4], refs[4:8], refs[8:]

    @pl.when(pl.program_id(0) == 0)
    def _():
        high, low = (first_ref[0, :, at : at + 1].astype(jnp.float32) for at in (0, 64))
        fill_bias((high * 256.0 + low).astype(jnp.int32), bias_ref)

    keep = (lax.axis_index("section") > 0).astype(jnp.float32)
    keys = stacked(key_refs)
    values = jnp.concatenate(
        [stacked(value_refs), jnp.ones((KEYS, HEAD_DIM), jnp.bfloat16)], axis=1
    )
    for index in range(GROUP):
        weights = weights_of(query_ref[0, :, head(index)], keys, bias_ref[...])
        mixed = jnp.dot(weights.astype(jnp.bfloat16), values, preferred_element_type=jnp.float32)
        result = mixed[:, :HEAD_DIM] * keep / mixed[:, HEAD_DIM:]
        out_ref[0, :, head(index)] = result.astype(jnp.bfloat16)


def probs_kernel(len_ref, query_ref, *refs):
    key_refs, (out_ref, bias_ref) = refs[:4], refs[4:]

    @pl.when(pl.program_id(0) == 0)
    def _():
        fill_bias(first_keys(len_ref), bias_ref)

    keys = stacked(key_refs)
    for first in range(0, GROUP, HEADS_AT_ONCE):
        queries = stack_heads(query_ref, first, HEADS_AT_ONCE)
        weights = weights_of(queries, keys, jnp.concatenate([bias_ref[...]] * HEADS_AT_ONCE, axis=0))
        total = jnp.sum(weights, axis=1, keepdims=True)
        out_ref[0, first * ROWS : (first + HEADS_AT_ONCE) * ROWS, :] = weights * (1.0 / total)


def backward_kernel(probs_ref, query_ref, grad_ref, *refs):
    key_refs, value_refs = refs[:4], refs[4:8]
    (
        out_ref, own_ref, middle_ref, near_ref, far_ref, queries_ref, grads_ref, scores_ref, low_ref
    ) = refs[-9:]
    last = lax.axis_size("section") - 1
    keep = (lax.axis_index("section") < last).astype(jnp.float32).astype(jnp.bfloat16)
    keys, values = stacked(key_refs), stacked(value_refs)
    queries_ref[...] = stack_heads(query_ref, 0, GROUP)
    grads_ref[...] = stack_heads(grad_ref, 0, GROUP) * keep
    for first in range(0, GROUP, HEADS_AT_ONCE):
        at = slice(first * ROWS, (first + HEADS_AT_ONCE) * ROWS)
        probs = probs_ref[0, at, :]
        d_prob = lax.dot_general(grads_ref[at, :], values, NT, preferred_element_type=jnp.float32)
        delta = jnp.sum(probs * d_prob, axis=1, keepdims=True)
        scores_ref[at, :] = (probs * (d_prob - delta)).astype(jnp.bfloat16)
        low_ref[at, :] = probs.astype(jnp.bfloat16)
    d_query = jnp.dot(scores_ref[...], keys, preferred_element_type=jnp.float32) * SCALE
    for index in range(GROUP):
        out_ref[0, :, head(index)] = d_query[index * ROWS : (index + 1) * ROWS].astype(
            jnp.bfloat16
        )
    d_key = jnp.dot(queries_ref[...].T, scores_ref[...], preferred_element_type=jnp.float32).T
    d_value = jnp.dot(grads_ref[...].T, low_ref[...], preferred_element_type=jnp.float32).T
    for piece, part_ref in enumerate((far_ref, middle_ref, near_ref, own_ref)):
        at = slice(piece * ROWS, (piece + 1) * ROWS)
        part_ref[0, :, :HEAD_DIM] = (d_key[at] * SCALE).astype(jnp.bfloat16)
        part_ref[0, :, HEAD_DIM:] = d_value[at].astype(jnp.bfloat16)


def small_call(
    kernel, operands, in_specs, shapes, out_specs, steps, limit=SMALL_VMEM, bytes_accessed=COST
):
    return pl.pallas_call(
        kernel,
        grid=(steps,),
        out_shape=[jax.ShapeDtypeStruct(shape, jnp.bfloat16) for shape in shapes],
        in_specs=in_specs,
        out_specs=out_specs,
        cost_estimate=cost(COST, bytes_accessed),
        compiler_params=params(limit),
    )(*operands)


def row_spec(width, steps, column=0):
    return pl.BlockSpec((1, ROWS // steps, width), lambda i: (0, i, column))


def pack_kernel(len_ref, key_fwd, value_fwd, key_bwd, value_bwd, fwd_ref, bwd_ref):
    for key_ref, value_ref, out_ref in (
        (key_fwd, value_fwd, fwd_ref),
        (key_bwd, value_bwd, bwd_ref),
    ):
        out_ref[0, :, :KV_WIDTH] = key_ref[0]
        out_ref[0, :, KV_WIDTH : 2 * KV_WIDTH] = value_ref[0]
    rows = ROWS // PACK_STEPS
    first = first_keys(len_ref, rows, pl.program_id(0) * rows)
    high = jnp.where(first >= 256, 1, 0)
    left = lax.broadcasted_iota(jnp.int32, (rows, ROWS), 1) < ROWS // 2
    coded = jnp.where(left, high, first - 256 * high)
    fwd_ref[0, :, 2 * KV_WIDTH :] = coded.astype(jnp.float32).astype(jnp.bfloat16)


def pack(lengths, *keys_and_values):
    widths = [2 * KV_WIDTH + ROWS, 2 * KV_WIDTH]
    return small_call(
        pack_kernel,
        (lengths, *keys_and_values),
        [pl.BlockSpec(memory_space=pltpu.SMEM)] + [row_spec(KV_WIDTH, PACK_STEPS)] * 4,
        [(1, ROWS, width) for width in widths],
        [row_spec(width, PACK_STEPS) for width in widths],
        PACK_STEPS,
        PACK_VMEM,
        PACK_COST,
    )


def folded(middles, fars, nears):
    sums = []
    for middle, far, near in zip(middles, fars, nears):
        total = middle.astype(jnp.float32) + far.astype(jnp.float32)
        total = total + jnp.where(second_core(), near.astype(jnp.float32), 0.0)
        sums.append(total.astype(jnp.bfloat16))
    return sums[0] if len(sums) == 1 else jnp.concatenate(sums, axis=2)


def group_spec(first):
    return pl.BlockSpec((1, ROWS, GROUP_WIDTH), lambda i: (0, 0, first + i))


def key_specs(first):
    return [pl.BlockSpec((1, ROWS, HEAD_DIM), lambda i: (0, 0, first + i))] * 4


def value_specs(first):
    return key_specs(KV_HEADS + first)


def forward(query, pieces):
    return pl.pallas_call(
        forward_kernel,
        grid=(KV_HEADS,),
        out_shape=jax.ShapeDtypeStruct(query.shape, jnp.bfloat16),
        in_specs=[
            pl.BlockSpec((1, ROWS, ROWS), lambda i: (0, 0, 2 * KV_HEADS)),
            group_spec(0),
        ]
        + key_specs(0)
        + value_specs(0),
        out_specs=group_spec(0),
        scratch_shapes=[pltpu.VMEM((ROWS, KEYS), jnp.float32)],
        cost_estimate=cost(COST, COST),
        compiler_params=params(VMEM),
    )(pieces[-1], query, *pieces, *pieces)


def probabilities(lengths, query, pieces):
    block = (1, GROUP * ROWS, KEYS)
    return pl.pallas_call(
        probs_kernel,
        grid=(KV_HEADS,),
        out_shape=jax.ShapeDtypeStruct((KV_HEADS,) + block[1:], jnp.float32),
        in_specs=[pl.BlockSpec(memory_space=pltpu.SMEM), group_spec(0)] + key_specs(0),
        out_specs=pl.BlockSpec(block, lambda i: (i, 0, 0)),
        scratch_shapes=[pltpu.VMEM((ROWS, KEYS), jnp.float32)],
        cost_estimate=cost(COST, COST),
        compiler_params=params(VMEM),
    )(lengths, query, *pieces)


def backward(probs, query, out_grad, pieces, first, groups, so_far):
    width = groups * 2 * HEAD_DIM
    in_specs = [pl.BlockSpec((1, GROUP * ROWS, KEYS), lambda i: (first + i, 0, 0))]
    in_specs += [group_spec(first)] * 2 + key_specs(first) + value_specs(first)
    operands = [probs, query, out_grad, *pieces, *pieces]
    aliases = {}
    if so_far is not None:
        in_specs.append(pl.BlockSpec(memory_space=pl.ANY))
        aliases = {len(operands): 0}
        operands.append(so_far)
    result = pl.pallas_call(
        backward_kernel,
        grid=(groups,),
        out_shape=[jax.ShapeDtypeStruct(query.shape, jnp.bfloat16)]
        + [jax.ShapeDtypeStruct((1, ROWS, width), jnp.bfloat16)] * 4,
        in_specs=in_specs,
        out_specs=[group_spec(first)]
        + [pl.BlockSpec((1, ROWS, 2 * HEAD_DIM), lambda i: (0, 0, i))] * 4,
        scratch_shapes=[
            pltpu.VMEM((GROUP * ROWS, HEAD_DIM), jnp.bfloat16),
            pltpu.VMEM((GROUP * ROWS, HEAD_DIM), jnp.bfloat16),
            pltpu.VMEM((GROUP * ROWS, KEYS), jnp.bfloat16),
            pltpu.VMEM((GROUP * ROWS, KEYS), jnp.bfloat16),
        ],
        input_output_aliases=aliases,
        cost_estimate=cost(COST, COST),
        compiler_params=params(VMEM),
    )(*operands)
    return result[0], result[1:]


def add_kernel(*refs):
    chunks = len(CHUNKS)
    own_refs, near_refs, fold_refs = refs[:chunks], refs[chunks : 2 * chunks], refs[2 * chunks : -2]
    key_ref, value_ref = refs[-2:]
    folds = [
        (ref, at)
        for ref, members in zip(fold_refs, FOLDS)
        for at in [sum(CHUNKS[chunk] for chunk in members[:spot]) for spot in range(len(members))]
    ]
    first = 0
    first_core = lax.rem(lax.axis_index("ctx"), 2) == 0
    for groups, own_ref, near_ref, (fold_ref, at) in zip(CHUNKS, own_refs, near_refs, folds):
        for group in range(groups):
            here = slice(2 * group * HEAD_DIM, 2 * (group + 1) * HEAD_DIM)
            there = slice(2 * (at + group) * HEAD_DIM, 2 * (at + group + 1) * HEAD_DIM)
            total = own_ref[0, :, here].astype(jnp.float32)
            near = near_ref[0, :, here].astype(jnp.float32)
            total = total + jnp.where(first_core, near, 0.0)
            total = (total + fold_ref[0, :, there].astype(jnp.float32)).astype(jnp.bfloat16)
            key_ref[0, :, head(first + group)] = total[:, :HEAD_DIM]
            value_ref[0, :, head(first + group)] = total[:, HEAD_DIM:]
        first += groups


def add_parts(*parts):
    return small_call(
        add_kernel,
        parts,
        [row_spec(part.shape[2], 1) for part in parts],
        [(1, ROWS, KV_WIDTH)] * 2,
        [row_spec(KV_WIDTH, 1)] * 2,
        1,
    )


def gather_behind(own, what, *earlier):
    middle = from_behind(after(own, *earlier), "ctx", 2, what + "_middle")
    far = from_behind(middle, "ctx", 1, what + "_far")
    near = swapped(jnp.where(second_core(), middle, own), what + "_near")
    return far, middle, near, own


def on_device(
    query_fwd,
    key_fwd,
    value_fwd,
    doc_len_fwd,
    query_bwd,
    key_bwd,
    value_bwd,
    doc_len_bwd,
    grad_held,
):
    out_grad = from_behind(grad_held, "section", -1, "grad")
    kv_fwd, own_bwd = pack(doc_len_fwd, key_fwd, value_fwd, key_bwd, value_bwd)
    own_fwd = from_behind(kv_fwd, "section", 1, "kv_moved")
    pieces_bwd = gather_behind(own_bwd, "kv_bwd", kv_fwd)
    query_moved = from_behind(after(query_fwd, own_fwd), "section", 1, "query_moved")
    probs = probabilities(doc_len_bwd, query_bwd, pieces_bwd)
    pieces_fwd = gather_behind(own_fwd, "kv_fwd", probs)
    grad_query = None
    first = 0
    owns, middles, nears, fars, folds = [], [], [], [], []
    for chunk, groups in enumerate(CHUNKS):
        grad_query, (own, middle, near, far) = backward(
            probs, query_bwd, out_grad, pieces_bwd, first, groups, grad_query
        )
        first += groups
        if chunk > 0:
            far = after(far, fars[0])
        owns.append(own)
        middles.append(middle)
        fars.append(from_behind(far, "ctx", -1, f"part_far_{chunk}"))
        nears.append(swapped(near, f"part_near_{chunk}"))
    for members in FOLDS:
        fold = folded(*([values[chunk] for chunk in members] for values in (middles, fars, nears)))
        if members == FOLDS[-1]:
            fold = after(fold, query_moved)
        folds.append(from_behind(fold, "ctx", -2, f"part_fold_{members[0]}"))
    next_stream = forward(query_moved, pieces_fwd)
    grad_key, grad_value = add_parts(after(owns[0], next_stream), *owns[1:], *nears, *folds)
    return (next_stream, grad_query, grad_key, grad_value)


def solution(mesh):
    spec = P("section", "ctx", None)
    row = P("section", None)
    return jax.shard_map(
        on_device,
        mesh=mesh,
        in_specs=(spec, spec, spec, row, spec, spec, spec, row, spec),
        out_specs=(spec, spec, spec, spec),
        check_vma=False,
    )
```
